512 devices in a mesh: depth: 8 (over z_lo), row: 8 (over z_hi, x), col: 8 (over y, core).
Axes of the slice: x: 4, y: 4, z: 16 (z_hi: 2, z_lo: 8; z = z_hi * 8 + z_lo), core: 2. Of those that a mesh axis runs over, the one named last changes fastest.
Arguments:
- tokens: bfloat16 [512, 12288], P(('depth', 'col'), 'row'), may hold values from -6 to 6
- grad_out: bfloat16 [512, 12288], P(('depth', 'col'), 'row'), may hold values from -3 to 3
- w_up: bfloat16 [12288, 24576], P('row', ('depth', 'col')), may hold values from -0.0546875 to 0.0546875
- w_down: bfloat16 [24576, 12288], P(('depth', 'col'), 'row'), may hold values from -0.0390625 to 0.0390625
Outputs:
- grad_tokens: bfloat16 [512, 12288], P(('depth', 'col'), 'row')
- grad_up: bfloat16 [12288, 24576], P('row', ('depth', 'col'))
- grad_down: bfloat16 [24576, 12288], P(('depth', 'col'), 'row')
The draws below stay inside these ranges and needn't reach their ends.
All inputs are finite; a program needn't handle non-finite values.
Results may differ from the reference program's by a relative error of at most 0.023.
Values may be sent and summed in bfloat16 or wider, within the bound.
No kernel may reach another device: no remote copies, remote signals or barrier semaphores. Data moves between devices by JAX's collectives and lax.ppermute only.
A program may use at most 64 MiB of HBM per device.

```python
import math
import jax
import jax.numpy as jnp
from jax import lax

D = 12288
FF = 24576
TOKENS = 512
N_ROW = 8


def level_of(key, dims, split, least, largest):
    gain, own = 1.0, jax.random.fold_in(key, 6)
    for axis_at, shards_of in split:
        draws = jnp.exp(jax.random.uniform(jax.random.fold_in(own, axis_at), (shards_of,), jnp.float32, least / len(split), largest / len(split)))
        gain = gain * jnp.repeat(draws, dims[axis_at] // shards_of).reshape([-1 if axis == axis_at else 1 for axis in range(len(dims))])
    return gain


def noise(key, shape, scale, most, pieces=(), held_as=jnp.bfloat16):
    level = level_of(key, shape, pieces, -0.22, 0.18) if pieces else 1.0
    array = jax.random.normal(key, shape, jnp.float32) * scale * level
    return jnp.minimum(jnp.maximum(array, -most), most).astype(held_as)


def setup_inputs(seed: int = 0) -> dict:
    keys = jax.random.split(jax.random.key(seed), 5)
    return {
        "tokens": noise(keys[0], (TOKENS, D), 1.0, 6.0, ((0, 64), (1, 8))),
        "grad_out": noise(keys[1], (TOKENS, D), 0.5, 3.0, ((0, 64), (1, 8))),
        "w_up": noise(keys[2], (D, FF), D ** -0.5, 0.0546875, ((0, 8), (1, 64))),
        "w_down": noise(keys[3], (FF, D), FF ** -0.5, 0.0390625, ((0, 64), (1, 8))),
    }


gelu_coef = 0.044715

def gelu_value(pre):
    inner = math.sqrt(2.0 / math.pi) * (pre + gelu_coef * pre * pre * pre)
    return 0.5 * pre * (1.0 + jnp.tanh(inner))

def gelu_slope(pre):
    scale = math.sqrt(2.0 / math.pi)
    tanh_val = jnp.tanh(scale * (pre + gelu_coef * pre * pre * pre))
    return 0.5 * (1.0 + tanh_val) + 0.5 * pre * (1.0 - tanh_val * tanh_val) * scale * (1.0 + 3.0 * gelu_coef * pre * pre)

def reference(tokens, grad_out, w_up, w_down):
    width = D // N_ROW
    pre_act = jnp.zeros((TOKENS, FF), jnp.float32)
    grad_act = jnp.zeros((TOKENS, FF), jnp.float32)
    for block in range(N_ROW):
        lower = block * width
        part_up = jnp.dot(tokens[:, lower:lower + width], w_up[lower:lower + width, :], preferred_element_type=jnp.float32)
        part_up = lax.optimization_barrier(part_up.astype(jnp.bfloat16))
        pre_act = pre_act + part_up.astype(jnp.float32)
        part_grad = lax.dot_general(grad_out[:, lower:lower + width], w_down[:, lower:lower + width], (((1,), (1,)), ((), ())), preferred_element_type=jnp.float32)
        part_grad = lax.optimization_barrier(part_grad.astype(jnp.bfloat16))
        grad_act = grad_act + part_grad.astype(jnp.float32)
    activated = gelu_value(pre_act).astype(jnp.bfloat16)
    grad_pre = (grad_act * gelu_slope(pre_act)).astype(jnp.bfloat16)
    token_blocks = tokens.reshape(TOKENS, N_ROW, width).transpose(1, 0, 2)

    def up_block(piece):
        return lax.dot_general(piece, grad_pre, (((0,), (0,)), ((), ())), preferred_element_type=jnp.float32).astype(jnp.bfloat16)
    grad_up = lax.map(up_block, token_blocks).reshape(D, FF)
    hidden_blocks = activated.reshape(TOKENS, N_ROW, FF // N_ROW).transpose(1, 0, 2)

    def down_block(piece):
        return lax.dot_general(piece, grad_out, (((0,), (0,)), ((), ())), preferred_element_type=jnp.float32).astype(jnp.bfloat16)
    grad_down = lax.map(down_block, hidden_blocks).reshape(FF, D)
    grad_tokens = lax.dot_general(grad_pre, w_up, (((1,), (1,)), ((), ())), preferred_element_type=jnp.float32).astype(jnp.bfloat16)
    return (grad_tokens, grad_up, grad_down)
```

```python
import math

import jax
import jax.numpy as jnp
from jax import lax
from jax.sharding import Mesh
from jax.sharding import PartitionSpec as P

gelu_coef = 0.044715
bf16, f32 = jnp.bfloat16, jnp.float32


def gelu_both(pre):
    scale = math.sqrt(2.0 / math.pi)
    tanh_val = jnp.tanh(scale * (pre + gelu_coef * pre * pre * pre))
    value = 0.5 * pre * (1.0 + tanh_val)
    slope = 0.5 * (1.0 + tanh_val) + 0.5 * pre * (1.0 - tanh_val * tanh_val) * scale * (
        1.0 + 3.0 * gelu_coef * pre * pre
    )
    return value, slope


def gather(part, axis):
    n = lax.axis_size(axis)
    return lax.all_to_all(jnp.broadcast_to(part[None], (n, *part.shape)), axis, 0, 0, tiled=True)


def swap(part, axis):
    return lax.ppermute(part, axis, [(0, 1), (1, 0)])


def scatter_sum(parts, axis):
    return lax.all_to_all(parts, axis, 0, 0, tiled=True).astype(f32).sum(0)


def dot(a, b, dims):
    return lax.dot_general(a, b, (dims, ((), ())), preferred_element_type=f32)


def on_device(tokens, grad_out, w_up, w_down):
    rows, width = tokens.shape
    hidden = w_up.shape[1]
    nz, ny, nx = lax.axis_size("depth"), lax.axis_size("y"), lax.axis_size("x")
    both = jnp.stack([tokens, grad_out])
    mine = gather(gather(both, "depth"), "y")
    other = swap(mine, "core")
    half = ny * nz * rows

    def pick(k):
        return [piece[:, :, k].reshape(half, width) for piece in (mine, other)]

    all_tokens = jnp.concatenate(pick(0))
    all_grads = jnp.concatenate(pick(1))
    part_up = dot(all_tokens, w_up, ((1,), (0,))).astype(bf16)
    part_grad = dot(all_grads, w_down, ((1,), (1,))).astype(bf16)
    share = 2 * half // nx
    parts = jnp.stack([part_up.reshape(nx, share, hidden), part_grad.reshape(nx, share, hidden)], 1)
    sums = scatter_sum(parts, "x").astype(bf16)
    total = sums.astype(f32) + swap(sums, "zhi").astype(f32)
    value, slope = gelu_both(total[0])
    grad_pre = gather((total[1] * slope).astype(bf16), "x").reshape(2 * half, hidden)
    activated = gather(value.astype(bf16), "x").reshape(2 * half, hidden)
    theirs = dot(grad_pre[half:], w_up, ((1,), (1,))).astype(bf16)
    ours = dot(grad_pre[:half], w_up, ((1,), (1,)))
    part = (ours + swap(theirs, "core").astype(f32)).astype(bf16)
    part = scatter_sum(part.reshape(ny, nz * rows, width), "y").astype(bf16)
    grad_tokens = scatter_sum(part.reshape(nz, rows, width), "depth").astype(bf16)
    grad_up = dot(all_tokens, grad_pre, ((0,), (0,))).astype(bf16)
    grad_down = dot(activated, all_grads, ((0,), (0,))).astype(bf16)
    return (grad_tokens, grad_up, grad_down)


def solution(mesh):
    fine = Mesh(mesh.devices.reshape(8, 2, 4, 4, 2), ("depth", "zhi", "x", "y", "core"))
    token, feature = ("depth", "y", "core"), ("zhi", "x")
    in_specs = (P(token, feature), P(token, feature), P(feature, token), P(token, feature))
    out_specs = (P(token, feature), P(feature, token), P(token, feature))
    return jax.shard_map(
        on_device, mesh=fine, in_specs=in_specs, out_specs=out_specs, check_vma=False
    )
```

```python
import math

import jax
import jax.numpy as jnp
from jax import lax
from jax.sharding import Mesh
from jax.sharding import PartitionSpec as P

gelu_coef = 0.044715
bf16, f32 = jnp.bfloat16, jnp.float32


def gelu_both(pre):
    scale = math.sqrt(2.0 / math.pi)
    tanh_val = jnp.tanh(scale * (pre + gelu_coef * pre * pre * pre))
    value = 0.5 * pre * (1.0 + tanh_val)
    slope = 0.5 * (1.0 + tanh_val) + 0.5 * pre * (1.0 - tanh_val * tanh_val) * scale * (
        1.0 + 3.0 * gelu_coef * pre * pre
    )
    return value, slope


def gather(part, axis):
    n = lax.axis_size(axis)
    return lax.all_to_all(jnp.broadcast_to(part[None], (n, *part.shape)), axis, 0, 0, tiled=True)


def swap(part, axis):
    return lax.ppermute(part, axis, [(0, 1), (1, 0)])


def scatter_sum(parts, axis):
    return lax.all_to_all(parts, axis, 0, 0, tiled=True).astype(f32).sum(0)


def dot(a, b, dims):
    return lax.dot_general(a, b, (dims, ((), ())), preferred_element_type=f32)


def on_device(tokens, grad_out, w_up, w_down):
    rows, width = tokens.shape
    hidden = w_up.shape[1]
    nz, ny, nx = lax.axis_size("depth"), lax.axis_size("y"), lax.axis_size("x")
    half = ny * nz * rows
    share = 2 * half // nx

    def gather_all(part):
        mine = gather(gather(part, "depth"), "y")
        return jnp.concatenate([mine, swap(mine, "core")]).reshape(2 * half, width)

    def sum_row(part):
        sums = scatter_sum(part.astype(bf16).reshape(nx, share, hidden), "x").astype(bf16)
        return sums.astype(f32) + swap(sums, "zhi").astype(f32)

    all_tokens = gather_all(tokens)
    all_grads = gather_all(grad_out)
    pre_act = sum_row(dot(all_tokens, w_up, ((1,), (0,))))
    grad_act = sum_row(dot(all_grads, w_down, ((1,), (1,))))
    value, slope = gelu_both(pre_act)
    activated = gather(value.astype(bf16), "x").reshape(2 * half, hidden)
    grad_pre = gather((grad_act * slope).astype(bf16), "x").reshape(2 * half, hidden)
    theirs = dot(grad_pre[half:], w_up, ((1,), (1,))).astype(bf16)
    ours = dot(grad_pre[:half], w_up, ((1,), (1,)))
    part = (ours + swap(theirs, "core").astype(f32)).astype(bf16)
    part = scatter_sum(part.reshape(ny, nz * rows, width), "y").astype(bf16)
    grad_tokens = scatter_sum(part.reshape(nz, rows, width), "depth").astype(bf16)
    grad_up = dot(all_tokens, grad_pre, ((0,), (0,))).astype(bf16)
    grad_down = dot(activated, all_grads, ((0,), (0,))).astype(bf16)
    return (grad_tokens, grad_up, grad_down)


def solution(mesh):
    fine = Mesh(mesh.devices.reshape(8, 2, 4, 4, 2), ("depth", "zhi", "x", "y", "core"))
    token, feature = ("depth", "y", "core"), ("zhi", "x")
    in_specs = (P(token, feature), P(token, feature), P(feature, token), P(token, feature))
    out_specs = (P(token, feature), P(feature, token), P(token, feature))
    return jax.shard_map(
        on_device, mesh=fine, in_specs=in_specs, out_specs=out_specs, check_vma=False
    )
```

```python
import math

import jax
import jax.numpy as jnp
from jax import lax
from jax.sharding import Mesh
from jax.sharding import PartitionSpec as P

gelu_coef = 0.044715
bf16, f32 = jnp.bfloat16, jnp.float32


def gelu_both(pre):
    scale = math.sqrt(2.0 / math.pi)
    tanh_val = jnp.tanh(scale * (pre + gelu_coef * pre * pre * pre))
    value = 0.5 * pre * (1.0 + tanh_val)
    slope = 0.5 * (1.0 + tanh_val) + 0.5 * pre * (1.0 - tanh_val * tanh_val) * scale * (
        1.0 + 3.0 * gelu_coef * pre * pre
    )
    return value, slope


def gather(part, axis):
    n = lax.axis_size(axis)
    return lax.all_to_all(jnp.broadcast_to(part[None], (n, *part.shape)), axis, 0, 0, tiled=True)


def swap(part, axis):
    return lax.ppermute(part, axis, [(0, 1), (1, 0)])


def scatter_sum(parts, axis):
    return lax.all_to_all(parts, axis, 0, 0, tiled=True).astype(f32).sum(0)


def dot(a, b, dims):
    return lax.dot_general(a, b, (dims, ((), ())), preferred_element_type=f32)


def on_device(tokens, grad_out, w_up, w_down):
    rows, width = tokens.shape
    hidden = w_up.shape[1]
    nz, ny, nx = lax.axis_size("depth"), lax.axis_size("y"), lax.axis_size("x")
    count, block = 2 * ny * nz * rows, nz * rows
    core = lax.axis_index("core")
    both = gather(jnp.stack([tokens, grad_out]), "depth")

    def sum_row(part):
        return scatter_sum(part.astype(bf16).reshape(nx, count // nx, hidden), "x").astype(bf16)

    def add_row(sums):
        return sums.astype(f32) + swap(sums, "zhi").astype(f32)

    all_grads = lax.all_gather(both[:, 1].reshape(block, width), ("y", "core"), axis=0, tiled=True)
    mine = gather(both[:, 0].reshape(block, width), "y")
    other = swap(mine, "core")
    all_tokens = jnp.where(
        core == 0, jnp.stack([mine, other], 1), jnp.stack([other, mine], 1)
    ).reshape(count, width)
    pre_sums = sum_row(dot(all_tokens, w_up, ((1,), (0,))))
    pre_sums, all_grads = lax.optimization_barrier((pre_sums, all_grads))
    pre_act = add_row(pre_sums)
    grad_sums = sum_row(dot(all_grads, w_down, ((1,), (1,))))
    value, slope = gelu_both(pre_act)
    activated = gather(value.astype(bf16), "x").reshape(count, hidden)
    grad_act = add_row(grad_sums)
    activated, grad_act = lax.optimization_barrier((activated, grad_act))
    grad_pre = gather((grad_act * slope).astype(bf16), "x").reshape(count, hidden)
    halves = grad_pre.reshape(ny, 2, block, hidden)

    def half(k):
        rows_of = lax.dynamic_index_in_dim(halves, k, 1, keepdims=False)
        return dot(rows_of.reshape(ny * block, hidden), w_up, ((1,), (1,)))

    theirs = half(1 - core).astype(bf16)
    part = (half(core) + swap(theirs, "core").astype(f32)).astype(bf16)
    part = scatter_sum(part.reshape(ny, block, width), "y").astype(bf16)
    grad_tokens = scatter_sum(part.reshape(nz, rows, width), "depth").astype(bf16)
    grad_up = dot(all_tokens, grad_pre, ((0,), (0,))).astype(bf16)
    grad_down = dot(activated, all_grads, ((0,), (0,))).astype(bf16)
    return (grad_tokens, grad_up, grad_down)


def solution(mesh):
    fine = Mesh(mesh.devices.reshape(8, 2, 4, 4, 2), ("depth", "zhi", "x", "y", "core"))
    token, feature = ("depth", "y", "core"), ("zhi", "x")
    in_specs = (P(token, feature), P(token, feature), P(feature, token), P(token, feature))
    out_specs = (P(token, feature), P(feature, token), P(token, feature))
    return jax.shard_map(
        on_device, mesh=fine, in_specs=in_specs, out_specs=out_specs, check_vma=False
    )
```

```python
import math

import jax
import jax.numpy as jnp
from jax import lax
from jax.sharding import Mesh
from jax.sharding import PartitionSpec as P

gelu_coef = 0.044715
bf16, f32 = jnp.bfloat16, jnp.float32


def gelu_both(pre):
    scale = math.sqrt(2.0 / math.pi)
    tanh_val = jnp.tanh(scale * (pre + gelu_coef * pre * pre * pre))
    value = 0.5 * pre * (1.0 + tanh_val)
    slope = 0.5 * (1.0 + tanh_val) + 0.5 * pre * (1.0 - tanh_val * tanh_val) * scale * (
        1.0 + 3.0 * gelu_coef * pre * pre
    )
    return value, slope


def gather(part, axis):
    n = lax.axis_size(axis)
    return lax.all_to_all(jnp.broadcast_to(part[None], (n, *part.shape)), axis, 0, 0, tiled=True)


def swap(part, axis):
    return lax.ppermute(part, axis, [(0, 1), (1, 0)])


def scatter_sum(parts, axis):
    return lax.all_to_all(parts, axis, 0, 0, tiled=True).astype(f32).sum(0)


def dot(a, b, dims):
    return lax.dot_general(a, b, (dims, ((), ())), preferred_element_type=f32)


def on_device(tokens, grad_out, w_up, w_down):
    rows, width = tokens.shape
    hidden = w_up.shape[1]
    nz, ny, nx = lax.axis_size("depth"), lax.axis_size("y"), lax.axis_size("x")
    both = jnp.stack([tokens, grad_out])
    mine = gather(gather(both, "depth"), "y")
    other = swap(mine, "core")
    half = ny * nz * rows

    def pick(k):
        return [piece[:, :, k].reshape(half, width) for piece in (mine, other)]

    all_tokens = jnp.concatenate(pick(0))
    all_grads = jnp.concatenate(pick(1))
    part_up = dot(all_tokens, w_up, ((1,), (0,))).astype(bf16)
    part_grad = dot(all_grads, w_down, ((1,), (1,))).astype(bf16)
    share = 2 * half // nx
    parts = jnp.stack([part_up.reshape(nx, share, hidden), part_grad.reshape(nx, share, hidden)], 1)
    sums = scatter_sum(parts, "x").astype(bf16)
    total = lax.all_gather(sums, "zhi").astype(f32).sum(0)
    value, slope = gelu_both(total[0])
    shares = jnp.stack([(total[1] * slope).astype(bf16), value.astype(bf16)])
    shares = gather(shares, "x")
    grad_pre, activated = (shares[:, k].reshape(2 * half, hidden) for k in (0, 1))
    theirs = dot(grad_pre[half:], w_up, ((1,), (1,))).astype(bf16)
    ours = dot(grad_pre[:half], w_up, ((1,), (1,)))
    part = (ours + swap(theirs, "core").astype(f32)).astype(bf16)
    part = scatter_sum(part.reshape(ny, nz * rows, width), "y").astype(bf16)
    grad_tokens = scatter_sum(part.reshape(nz, rows, width), "depth").astype(bf16)
    grad_up = dot(all_tokens, grad_pre, ((0,), (0,))).astype(bf16)
    grad_down = dot(activated, all_grads, ((0,), (0,))).astype(bf16)
    return (grad_tokens, grad_up, grad_down)


def solution(mesh):
    fine = Mesh(mesh.devices.reshape(8, 2, 4, 4, 2), ("depth", "zhi", "x", "y", "core"))
    token, feature = ("depth", "y", "core"), ("zhi", "x")
    in_specs = (P(token, feature), P(token, feature), P(feature, token), P(token, feature))
    out_specs = (P(token, feature), P(feature, token), P(token, feature))
    return jax.shard_map(
        on_device, mesh=fine, in_specs=in_specs, out_specs=out_specs, check_vma=False
    )
```

```python
import math

import jax
import jax.numpy as jnp
from jax import lax
from jax.sharding import Mesh
from jax.sharding import PartitionSpec as P

gelu_coef = 0.044715
bf16, f32 = jnp.bfloat16, jnp.float32


def gelu_both(pre):
    scale = math.sqrt(2.0 / math.pi)
    tanh_val = jnp.tanh(scale * (pre + gelu_coef * pre * pre * pre))
    value = 0.5 * pre * (1.0 + tanh_val)
    slope = 0.5 * (1.0 + tanh_val) + 0.5 * pre * (1.0 - tanh_val * tanh_val) * scale * (
        1.0 + 3.0 * gelu_coef * pre * pre
    )
    return value, slope


def gather(part, axis):
    n = lax.axis_size(axis)
    return lax.all_to_all(jnp.broadcast_to(part[None], (n, *part.shape)), axis, 0, 0, tiled=True)


def swap(part, axis):
    return lax.ppermute(part, axis, [(0, 1), (1, 0)])


def scatter_sum(parts, axis):
    return lax.all_to_all(parts, axis, 0, 0, tiled=True).astype(f32).sum(0)


def dot(a, b, dims):
    return lax.dot_general(a, b, (dims, ((), ())), preferred_element_type=f32)


def on_device(tokens, grad_out, w_up, w_down):
    rows, width = tokens.shape
    hidden = w_up.shape[1]
    ny, nx, nq = lax.axis_size("y"), lax.axis_size("x"), lax.axis_size("zq")
    both = gather(jnp.stack([tokens, grad_out]), "zq").swapaxes(0, 1)
    beside = swap(both, "zp")
    mine = gather(both, "y"), gather(beside, "y")
    other = swap(mine[0], "core"), swap(mine[1], "core")
    half = ny * 2 * nq * rows

    def pick(k):
        return [
            jnp.stack([piece[:, k] for piece in pair], 1).reshape(half, width)
            for pair in (mine, other)
        ]

    all_tokens = jnp.concatenate(pick(0))
    all_grads = jnp.concatenate(pick(1))
    part_up = dot(all_tokens, w_up, ((1,), (0,))).astype(bf16)
    part_grad = dot(all_grads, w_down, ((1,), (1,))).astype(bf16)
    share = 2 * half // nx
    parts = jnp.stack([part_up.reshape(nx, share, hidden), part_grad.reshape(nx, share, hidden)], 1)
    sums = scatter_sum(parts, "x").astype(bf16)
    total = lax.all_gather(sums, "zhi").astype(f32).sum(0)
    value, slope = gelu_both(total[0])
    shares = jnp.stack([(total[1] * slope).astype(bf16), value.astype(bf16)])
    shares = gather(shares, "x")
    grad_pre, activated = (shares[:, k].reshape(2 * half, hidden) for k in (0, 1))
    theirs = dot(grad_pre[half:], w_up, ((1,), (1,))).astype(bf16)
    ours = dot(grad_pre[:half], w_up, ((1,), (1,)))
    part = (ours + swap(theirs, "core").astype(f32)).astype(bf16)
    part = scatter_sum(part.reshape(ny, 2, nq, rows, width), "y").astype(bf16)
    part = jnp.where(lax.axis_index("zp") == 0, part, part[::-1]).swapaxes(0, 1)
    part = part.reshape(nq * 2, rows, width)
    grad_tokens = scatter_sum(part, ("zq", "zp")).astype(bf16)
    grad_up = dot(all_tokens, grad_pre, ((0,), (0,))).astype(bf16)
    grad_down = dot(activated, all_grads, ((0,), (0,))).astype(bf16)
    return (grad_tokens, grad_up, grad_down)


def solution(mesh):
    names = ("zq", "zp", "zhi", "x", "y", "core")
    fine = Mesh(mesh.devices.reshape(4, 2, 2, 4, 4, 2), names)
    token, feature = ("zq", "zp", "y", "core"), ("zhi", "x")
    in_specs = (P(token, feature), P(token, feature), P(feature, token), P(token, feature))
    out_specs = (P(token, feature), P(feature, token), P(token, feature))
    return jax.shard_map(
        on_device, mesh=fine, in_specs=in_specs, out_specs=out_specs, check_vma=False
    )
```

```python
import math

import jax
import jax.numpy as jnp
from jax import lax
from jax.sharding import Mesh
from jax.sharding import PartitionSpec as P

gelu_coef = 0.044715
bf16, f32 = jnp.bfloat16, jnp.float32


def gelu_both(pre):
    scale = math.sqrt(2.0 / math.pi)
    tanh_val = jnp.tanh(scale * (pre + gelu_coef * pre * pre * pre))
    value = 0.5 * pre * (1.0 + tanh_val)
    slope = 0.5 * (1.0 + tanh_val) + 0.5 * pre * (1.0 - tanh_val * tanh_val) * scale * (
        1.0 + 3.0 * gelu_coef * pre * pre
    )
    return value, slope


def gather(part, axis):
    n = lax.axis_size(axis)
    return lax.all_to_all(jnp.broadcast_to(part[None], (n, *part.shape)), axis, 0, 0, tiled=True)


def swap(part, axis):
    return lax.ppermute(part, axis, [(0, 1), (1, 0)])


def scatter_sum(parts, axis):
    return lax.all_to_all(parts, axis, 0, 0, tiled=True).astype(f32).sum(0)


def dot(a, b, dims):
    return lax.dot_general(a, b, (dims, ((), ())), preferred_element_type=f32)


def on_device(tokens, grad_out, w_up, w_down):
    rows, width = tokens.shape
    hidden = w_up.shape[1]
    nz, ny, nx = lax.axis_size("depth"), lax.axis_size("y"), lax.axis_size("x")
    half = ny * nz * rows
    up_all = jnp.concatenate([w_up, swap(w_up, "core")], 1)
    down_all = jnp.concatenate([w_down, swap(w_down, "core")], 0)
    mine = gather(gather(jnp.stack([tokens, grad_out]), "depth"), "y")
    my_tokens, my_grads = (mine[:, :, k].reshape(half, width) for k in (0, 1))
    part_up = dot(my_tokens, up_all, ((1,), (0,))).astype(bf16)
    part_grad = dot(my_grads, down_all, ((1,), (1,))).astype(bf16)
    share = half // nx
    parts = jnp.stack([part.reshape(nx, share, 2 * hidden) for part in (part_up, part_grad)], 1)
    sums = scatter_sum(parts, "x").astype(bf16)
    total = lax.all_gather(sums, "zhi").astype(f32).sum(0)
    value, slope = gelu_both(total[0])
    shares = jnp.stack([(total[1] * slope).astype(bf16), value.astype(bf16)])
    shares = gather(shares, "x")
    grad_pre, activated = (shares[:, k].reshape(half, 2 * hidden) for k in (0, 1))
    part = dot(grad_pre, up_all, ((1,), (1,))).astype(bf16)
    part = scatter_sum(part.reshape(ny, nz * rows, width), "y").astype(bf16)
    grad_tokens = scatter_sum(part.reshape(nz, rows, width), "depth").astype(bf16)
    other = swap(mine, "core")
    other_tokens, other_grads = (other[:, :, k].reshape(half, width) for k in (0, 1))
    theirs = swap(jnp.stack([grad_pre[:, hidden:], activated[:, hidden:]]), "core")
    over = ((0,), (0,))
    grad_up = dot(my_tokens, grad_pre[:, :hidden], over) + dot(other_tokens, theirs[0], over)
    grad_down = dot(activated[:, :hidden], my_grads, over) + dot(theirs[1], other_grads, over)
    return (grad_tokens, grad_up.astype(bf16), grad_down.astype(bf16))


def solution(mesh):
    fine = Mesh(mesh.devices.reshape(8, 2, 4, 4, 2), ("depth", "zhi", "x", "y", "core"))
    token, feature = ("depth", "y", "core"), ("zhi", "x")
    in_specs = (P(token, feature), P(token, feature), P(feature, token), P(token, feature))
    out_specs = (P(token, feature), P(feature, token), P(token, feature))
    return jax.shard_map(
        on_device, mesh=fine, in_specs=in_specs, out_specs=out_specs, check_vma=False
    )
```

```python
import math

import jax
import jax.numpy as jnp
from jax import lax
from jax.sharding import Mesh
from jax.sharding import PartitionSpec as P

gelu_coef = 0.044715
bf16, f32 = jnp.bfloat16, jnp.float32


def gelu_both(pre):
    scale = math.sqrt(2.0 / math.pi)
    tanh_val = jnp.tanh(scale * (pre + gelu_coef * pre * pre * pre))
    value = 0.5 * pre * (1.0 + tanh_val)
    slope = 0.5 * (1.0 + tanh_val) + 0.5 * pre * (1.0 - tanh_val * tanh_val) * scale * (
        1.0 + 3.0 * gelu_coef * pre * pre
    )
    return value, slope


def gather(part, axis):
    n = lax.axis_size(axis)
    return lax.all_to_all(jnp.broadcast_to(part[None], (n, *part.shape)), axis, 0, 0, tiled=True)


def swap(part, axis):
    return lax.ppermute(part, axis, [(0, 1), (1, 0)])


def scatter_sum(parts, axis):
    return lax.all_to_all(parts, axis, 0, 0, tiled=True).astype(f32).sum(0)


def dot(a, b, dims):
    return lax.dot_general(a, b, (dims, ((), ())), preferred_element_type=f32)


def on_device(tokens, grad_out, w_up, w_down):
    rows, width = tokens.shape
    hidden = w_up.shape[1]
    ny, nq = lax.axis_size("y"), lax.axis_size("zq")
    half, block = ny * 2 * nq * rows, nq * rows
    ups, downs = (w_up, swap(w_up, "core")), (w_down, swap(w_down, "core"))
    both = gather(jnp.stack([tokens, grad_out]), "zq").swapaxes(0, 1)
    pieces = gather(both, "y"), gather(swap(both, "zp"), "y")

    def first_dots(piece):
        left, right = (piece[:, k].reshape(ny * block, width) for k in (0, 1))
        parts = [dot(left, w, ((1,), (0,))) for w in ups] + [dot(right, w, ((1,), (1,))) for w in downs]
        return [part.astype(bf16).reshape(ny, block, hidden) for part in parts]

    parts = [jnp.stack(pair, 1) for pair in zip(*map(first_dots, pieces))]
    parts = jnp.stack(parts, 1).reshape(ny, 4, 2 * block, hidden)
    sums = scatter_sum(parts, "x").astype(bf16)
    total = lax.all_gather(sums, "zhi").astype(f32).sum(0)
    value, slope = gelu_both(total[:2])
    shares = jnp.concatenate([(total[2:] * slope).astype(bf16), value.astype(bf16)])
    shares = gather(shares, "x")
    grad_pre, grad_pre_other, activated, activated_other = (
        shares[:, k].reshape(half, hidden) for k in range(4)
    )
    part = dot(grad_pre, ups[0], ((1,), (1,))) + dot(grad_pre_other, ups[1], ((1,), (1,)))
    part = scatter_sum(part.astype(bf16).reshape(ny, 2, nq, rows, width), "y")
    part = jnp.where(lax.axis_index("zp") == 0, part, part[::-1]).astype(bf16)
    grad_tokens = scatter_sum(part.reshape(2 * nq, rows, width), ("zp", "zq")).astype(bf16)
    others = swap(pieces[0], "core"), swap(pieces[1], "core")

    def pick(k):
        kept = [jnp.stack([p[:, k] for p in pair], 1).reshape(half, width) for pair in (pieces, others)]
        return jnp.concatenate(kept)

    theirs = swap(jnp.stack([grad_pre_other, activated_other]), "core")
    over = ((0,), (0,))
    grad_up = dot(pick(0), jnp.concatenate([grad_pre, theirs[0]]), over)
    grad_down = dot(jnp.concatenate([activated, theirs[1]]), pick(1), over)
    return (grad_tokens, grad_up.astype(bf16), grad_down.astype(bf16))


def solution(mesh):
    names = ("zq", "zp", "zhi", "x", "y", "core")
    fine = Mesh(mesh.devices.reshape(4, 2, 2, 4, 4, 2), names)
    token, feature = ("zq", "zp", "y", "core"), ("zhi", "x")
    in_specs = (P(token, feature), P(token, feature), P(feature, token), P(token, feature))
    out_specs = (P(token, feature), P(feature, token), P(token, feature))
    return jax.shard_map(
        on_device, mesh=fine, in_specs=in_specs, out_specs=out_specs, check_vma=False
    )
```

```python
import math

import jax
import jax.numpy as jnp
from jax import lax
from jax.experimental import pallas as pl
from jax.experimental.pallas import tpu as pltpu
from jax.sharding import Mesh
from jax.sharding import PartitionSpec as P

gelu_coef = 0.044715
bf16, f32 = jnp.bfloat16, jnp.float32


def gelu_both(pre):
    scale = math.sqrt(2.0 / math.pi)
    tanh_val = jnp.tanh(scale * (pre + gelu_coef * pre * pre * pre))
    value = 0.5 * pre * (1.0 + tanh_val)
    slope = 0.5 * (1.0 + tanh_val) + 0.5 * pre * (1.0 - tanh_val * tanh_val) * scale * (
        1.0 + 3.0 * gelu_coef * pre * pre
    )
    return value, slope


def gather(part, axis):
    n = lax.axis_size(axis)
    return lax.all_to_all(jnp.broadcast_to(part[None], (n, *part.shape)), axis, 0, 0, tiled=True)


def swap(part, axis):
    return lax.ppermute(part, axis, [(0, 1), (1, 0)])


def scatter_sum(parts, axis):
    return lax.all_to_all(parts, axis, 0, 0, tiled=True).astype(f32).sum(0)


def dot(a, b, dims):
    return lax.dot_general(a, b, (dims, ((), ())), preferred_element_type=f32)


def first_kernel(near_ref, far_ref, *refs):
    weights, out_ref, held, done = refs[:4], refs[4], refs[5:9], refs[9]
    copies = [pltpu.make_async_copy(w, h, done.at[i]) for i, (w, h) in enumerate(zip(weights, held))]
    for copy in copies:
        copy.start()
    ny, _, block, width = near_ref.shape
    for k in range(2):
        rows = [ref[:, k].reshape(ny * block, width) for ref in (near_ref, far_ref)]
        rows = jnp.concatenate(rows, 0)
        for i in (2 * k, 2 * k + 1):
            copies[i].wait()
            part = dot(rows, held[i][...], ((1,), (k,))).astype(bf16)
            for p in range(2):
                piece = part[p * ny * block : (p + 1) * ny * block]
                out_ref[:, i, p] = piece.reshape(ny, block, piece.shape[1])


def first_dots(near, far, ups, downs):
    ny, _, block, width = near.shape
    weights = (*ups, *downs)
    hidden = ups[0].shape[1]
    vmem, anywhere = pl.BlockSpec(memory_space=pltpu.VMEM), pl.BlockSpec(memory_space=pl.ANY)
    return pl.pallas_call(
        first_kernel,
        out_shape=jax.ShapeDtypeStruct((ny, 4, 2, block, hidden), bf16),
        in_specs=[vmem, vmem] + [anywhere] * 4,
        out_specs=vmem,
        scratch_shapes=[pltpu.VMEM(w.shape, bf16) for w in weights] + [pltpu.SemaphoreType.DMA((4,))],
        compiler_params=pltpu.CompilerParams(vmem_limit_bytes=24 * 2**20),
        cost_estimate=pl.CostEstimate(
            flops=16 * ny * block * width * hidden, bytes_accessed=8 * 2**20, transcendentals=0
        ),
    )(near, far, *weights)


def sum_kernel(parts_ref, out_ref):
    total = parts_ref[0].astype(f32)
    for i in range(1, parts_ref.shape[0]):
        total += parts_ref[i].astype(f32)
    out_ref[...] = total.astype(out_ref.dtype)


def local_sum(parts):
    return pl.pallas_call(
        sum_kernel,
        out_shape=jax.ShapeDtypeStruct(parts.shape[1:], bf16),
        compiler_params=pltpu.CompilerParams(vmem_limit_bytes=16 * 2**20),
        cost_estimate=pl.CostEstimate(
            flops=parts.size, bytes_accessed=3 * parts.size, transcendentals=0
        ),
    )(parts)


def last_kernel(shares_ref, own_ref, other_ref, out_ref):
    nx, _, rows, hidden = shares_ref.shape
    total = 0.0
    for k, w_ref in enumerate((own_ref, other_ref)):
        left = shares_ref[:, k].reshape(nx * rows, hidden)
        total += dot(left, w_ref[...], ((1,), (1,)))
    out_ref[...] = total.astype(bf16).reshape(out_ref.shape)


def last_dots(shares, own, other, steps=1):
    nx, _, rows, hidden = shares.shape
    width = own.shape[0]
    wide = width // steps
    w_spec = pl.BlockSpec((wide, hidden), lambda i: (i, 0))
    return pl.pallas_call(
        last_kernel,
        grid=(steps,),
        out_shape=jax.ShapeDtypeStruct((nx, rows, width), bf16),
        in_specs=[pl.BlockSpec((nx, 2, rows, hidden), lambda i: (0, 0, 0, 0)), w_spec, w_spec],
        out_specs=pl.BlockSpec((nx, rows, wide), lambda i: (0, 0, i)),
        compiler_params=pltpu.CompilerParams(vmem_limit_bytes=16 * 2**20),
        cost_estimate=pl.CostEstimate(
            flops=4 * nx * rows * hidden * width, bytes_accessed=4 * 2**20, transcendentals=0
        ),
    )(shares, own, other)


def on_device(tokens, grad_out, w_up, w_down):
    rows, width = tokens.shape
    hidden = w_up.shape[1]
    ny, nq = lax.axis_size("y"), lax.axis_size("zq")
    half, block = ny * 2 * nq * rows, nq * rows
    both = gather(jnp.stack([tokens, grad_out]), "zq").swapaxes(0, 1)
    late_up, late_down, both = lax.optimization_barrier((w_up, w_down, both))
    ups, downs = (w_up, swap(late_up, "core")), (w_down, swap(late_down, "core"))
    pieces = gather(both, "y"), gather(swap(both, "zp"), "y")

    near, far = (piece.reshape(ny, 2, block, width) for piece in pieces)
    parts = first_dots(near, far, ups, downs).reshape(ny, 4, 2 * block, hidden)
    sums = local_sum(lax.all_to_all(parts, "x", 0, 0, tiled=True))
    total = lax.all_gather(sums, "zhi").astype(f32).sum(0)
    value, slope = gelu_both(total[:2])
    shares = jnp.concatenate([(total[2:] * slope).astype(bf16), value.astype(bf16)])
    shares = gather(shares, "x")
    grad_pre, grad_pre_other, activated, activated_other = (
        shares[:, k].reshape(half, hidden) for k in range(4)
    )
    part = last_dots(shares, *ups)
    part = scatter_sum(part.reshape(ny, 2, nq, rows, width), "y")
    part = jnp.where(lax.axis_index("zp") == 0, part, part[::-1]).astype(bf16)
    grad_tokens = scatter_sum(part.reshape(2 * nq, rows, width), ("zp", "zq")).astype(bf16)
    others = swap(pieces[0], "core"), swap(pieces[1], "core")

    def pick(k):
        kept = [jnp.stack([p[:, k] for p in pair], 1).reshape(half, width) for pair in (pieces, others)]
        return jnp.concatenate(kept)

    theirs = swap(jnp.stack([grad_pre_other, activated_other]), "core")
    over = ((0,), (0,))
    grad_up = dot(pick(0), jnp.concatenate([grad_pre, theirs[0]]), over)
    grad_down = dot(jnp.concatenate([activated, theirs[1]]), pick(1), over)
    return (grad_tokens, grad_up.astype(bf16), grad_down.astype(bf16))


def solution(mesh):
    names = ("zq", "zp", "zhi", "x", "y", "core")
    fine = Mesh(mesh.devices.reshape(4, 2, 2, 4, 4, 2), names)
    token, feature = ("zq", "zp", "y", "core"), ("zhi", "x")
    in_specs = (P(token, feature), P(token, feature), P(feature, token), P(token, feature))
    out_specs = (P(token, feature), P(feature, token), P(token, feature))
    return jax.shard_map(
        on_device, mesh=fine, in_specs=in_specs, out_specs=out_specs, check_vma=False
    )
```

```python
import math

import jax
import jax.numpy as jnp
from jax import lax
from jax.experimental import pallas as pl
from jax.experimental.pallas import tpu as pltpu
from jax.sharding import Mesh
from jax.sharding import PartitionSpec as P

gelu_coef = 0.044715
bf16, f32 = jnp.bfloat16, jnp.float32


def gelu_both(pre):
    scale = math.sqrt(2.0 / math.pi)
    tanh_val = jnp.tanh(scale * (pre + gelu_coef * pre * pre * pre))
    value = 0.5 * pre * (1.0 + tanh_val)
    slope = 0.5 * (1.0 + tanh_val) + 0.5 * pre * (1.0 - tanh_val * tanh_val) * scale * (
        1.0 + 3.0 * gelu_coef * pre * pre
    )
    return value, slope


def gather(part, axis):
    n = lax.axis_size(axis)
    return lax.all_to_all(jnp.broadcast_to(part[None], (n, *part.shape)), axis, 0, 0, tiled=True)


def swap(part, axis):
    return lax.ppermute(part, axis, [(0, 1), (1, 0)])


def scatter_sum(parts, axis):
    return lax.all_to_all(parts, axis, 0, 0, tiled=True).astype(f32).sum(0)


def dot(a, b, dims):
    return lax.dot_general(a, b, (dims, ((), ())), preferred_element_type=f32)


def first_kernel(near_ref, far_ref, *refs):
    weights, out_ref, held, made, done = refs[:4], refs[4], refs[5:9], refs[9], refs[10]
    copies = [pltpu.make_async_copy(w, h, done.at[i]) for i, (w, h) in enumerate(zip(weights, held))]
    for copy in copies:
        copy.start()
    ny, _, block, width = near_ref.shape
    for k in range(2):
        rows = [ref[:, k].reshape(ny * block, width) for ref in (near_ref, far_ref)]
        rows = jnp.concatenate(rows, 0)
        for i in (2 * k, 2 * k + 1):
            copies[i].wait()
            part = dot(rows, held[i][...], ((1,), (k,))).astype(bf16)
            for p in range(2):
                piece = part[p * ny * block : (p + 1) * ny * block]
                made[i, :, p] = piece.reshape(ny, block, piece.shape[1])
            copies.append(pltpu.make_async_copy(made.at[i], out_ref.at[:, i], done.at[4 + i]))
            copies[-1].start()
    for copy in copies[4:]:
        copy.wait()


def first_dots(near, far, ups, downs):
    ny, _, block, width = near.shape
    weights = (*ups, *downs)
    hidden = ups[0].shape[1]
    vmem, anywhere = pl.BlockSpec(memory_space=pltpu.VMEM), pl.BlockSpec(memory_space=pl.ANY)
    return pl.pallas_call(
        first_kernel,
        out_shape=jax.ShapeDtypeStruct((ny, 4, 2, block, hidden), bf16),
        in_specs=[vmem, vmem] + [anywhere] * 4,
        out_specs=anywhere,
        scratch_shapes=[pltpu.VMEM(w.shape, bf16) for w in weights]
        + [pltpu.VMEM((4, ny, 2, block, hidden), bf16), pltpu.SemaphoreType.DMA((8,))],
        compiler_params=pltpu.CompilerParams(vmem_limit_bytes=24 * 2**20),
        cost_estimate=pl.CostEstimate(
            flops=16 * ny * block * width * hidden, bytes_accessed=8 * 2**20, transcendentals=0
        ),
    )(near, far, *weights)


def sum_kernel(parts_ref, out_ref):
    total = parts_ref[0].astype(f32)
    for i in range(1, parts_ref.shape[0]):
        total += parts_ref[i].astype(f32)
    out_ref[...] = total.astype(out_ref.dtype)


def local_sum(parts):
    return pl.pallas_call(
        sum_kernel,
        out_shape=jax.ShapeDtypeStruct(parts.shape[1:], bf16),
        compiler_params=pltpu.CompilerParams(vmem_limit_bytes=16 * 2**20),
        cost_estimate=pl.CostEstimate(
            flops=parts.size, bytes_accessed=3 * parts.size, transcendentals=0
        ),
    )(parts)


def last_kernel(shares_ref, own_ref, other_ref, out_ref):
    nx, _, rows, hidden = shares_ref.shape
    total = 0.0
    for k, w_ref in enumerate((own_ref, other_ref)):
        left = shares_ref[:, k].reshape(nx * rows, hidden)
        total += dot(left, w_ref[...], ((1,), (1,)))
    out_ref[...] = total.astype(bf16).reshape(out_ref.shape)


def last_dots(shares, own, other, steps=1):
    nx, _, rows, hidden = shares.shape
    width = own.shape[0]
    wide = width // steps
    w_spec = pl.BlockSpec((wide, hidden), lambda i: (i, 0))
    return pl.pallas_call(
        last_kernel,
        grid=(steps,),
        out_shape=jax.ShapeDtypeStruct((nx, rows, width), bf16),
        in_specs=[pl.BlockSpec((nx, 2, rows, hidden), lambda i: (0, 0, 0, 0)), w_spec, w_spec],
        out_specs=pl.BlockSpec((nx, rows, wide), lambda i: (0, 0, i)),
        compiler_params=pltpu.CompilerParams(vmem_limit_bytes=16 * 2**20),
        cost_estimate=pl.CostEstimate(
            flops=4 * nx * rows * hidden * width, bytes_accessed=4 * 2**20, transcendentals=0
        ),
    )(shares, own, other)


def on_device(tokens, grad_out, w_up, w_down):
    rows, width = tokens.shape
    hidden = w_up.shape[1]
    ny, nq = lax.axis_size("y"), lax.axis_size("zq")
    half, block = ny * 2 * nq * rows, nq * rows
    both = gather(jnp.stack([tokens, grad_out]), "zq").swapaxes(0, 1)
    late_up, late_down, both = lax.optimization_barrier((w_up, w_down, both))
    ups, downs = (w_up, swap(late_up, "core")), (w_down, swap(late_down, "core"))
    pieces = gather(both, "y"), gather(swap(both, "zp"), "y")

    near, far = (piece.reshape(ny, 2, block, width) for piece in pieces)
    parts = first_dots(near, far, ups, downs).reshape(ny, 4, 2 * block, hidden)
    sums = local_sum(lax.all_to_all(parts, "x", 0, 0, tiled=True))
    total = lax.all_gather(sums, "zhi").astype(f32).sum(0)
    value, slope = gelu_both(total[:2])
    shares = jnp.concatenate([(total[2:] * slope).astype(bf16), value.astype(bf16)])
    shares = gather(shares, "x")
    grad_pre, grad_pre_other, activated, activated_other = (
        shares[:, k].reshape(half, hidden) for k in range(4)
    )
    part = last_dots(shares, *ups)
    part = scatter_sum(part.reshape(ny, 2, nq, rows, width), "y")
    part = jnp.where(lax.axis_index("zp") == 0, part, part[::-1]).astype(bf16)
    grad_tokens = scatter_sum(part.reshape(2 * nq, rows, width), ("zp", "zq")).astype(bf16)
    others = swap(pieces[0], "core"), swap(pieces[1], "core")

    def pick(k):
        kept = [jnp.stack([p[:, k] for p in pair], 1).reshape(half, width) for pair in (pieces, others)]
        return jnp.concatenate(kept)

    theirs = swap(jnp.stack([grad_pre_other, activated_other]), "core")
    over = ((0,), (0,))
    grad_up = dot(pick(0), jnp.concatenate([grad_pre, theirs[0]]), over)
    grad_down = dot(jnp.concatenate([activated, theirs[1]]), pick(1), over)
    return (grad_tokens, grad_up.astype(bf16), grad_down.astype(bf16))


def solution(mesh):
    names = ("zq", "zp", "zhi", "x", "y", "core")
    fine = Mesh(mesh.devices.reshape(4, 2, 2, 4, 4, 2), names)
    token, feature = ("zq", "zp", "y", "core"), ("zhi", "x")
    in_specs = (P(token, feature), P(token, feature), P(feature, token), P(token, feature))
    out_specs = (P(token, feature), P(feature, token), P(token, feature))
    return jax.shard_map(
        on_device, mesh=fine, in_specs=in_specs, out_specs=out_specs, check_vma=False
    )
```
